32 devices in a mesh: tile: 8 (over z, y), lev: 4 (over x, core).
Axes of the slice: x: 2, y: 2, z: 4, core: 2. Of those that a mesh axis runs over, the one named last changes fastest.
Arguments:
- cotangent: bfloat16 [3072, 128, 128], P('lev', 'tile'), may hold values from -6 to 6
- mix_weight: bfloat16 [3072, 3072], P(None, 'tile'), may hold values from -0.109375 to 0.109375
- kernel: float32 [3072, 9], P('lev'), may hold values from -2 to 2
- send_rows: int32 [8, 8, 41], P('tile'), may hold values from -1 to 291, as said below
- recv_cells: int32 [8, 8, 41], P('tile'), may hold values from -1 to 1918, as said below
- recv_weight: float32 [8, 4, 8, 41], P('tile'), may hold values from 0 to 1, as said below
Outputs:
- grad_input: bfloat16 [3072, 128, 128], P('lev', 'tile')
The draws below stay inside these ranges and needn't reach their ends.
Inputs may be any that keep to these rules, and one draw needn't show every extreme that they name: `send_rows`: partner d is always a strip of the other panel. Every slot of the side columns (with the four corners) of strip s appears exactly once over all d and k, the slots of row 0 only for the strip at place 0 of a panel and those of row 17 only for the strip at place 4 - 1; no other slots appear. Used entries of a block come first, and some pair uses all 41. recv_cells[d, s, k] is -1 exactly where send_rows[s, d, k] is -1; otherwise its row is at most 14 and its column at most 126, so all four corners lie in strip d; the largest cell is reached. `recv_weight`: the four weights of an entry are the bilinear weights of a point in the donor cell and sum to one.
All inputs are finite; a program needn't handle non-finite values.
Results may differ from the reference program's by a relative error of at most 0.0049.
Values may be sent and summed in bfloat16 or wider, within the bound.
A program may use at most 128 MiB of HBM per device.

```python
import jax
import jax.numpy as jnp
from jax import lax

FEAT = 3072
BR = 16
BC = 128
NS = 4
ROWS = 128
RIM_SLOTS = 292
MOST = 41
N_TILE = 8


def donor_plan(key):
    base_key = jax.random.fold_in(key, 7)
    key_perm, key_row, key_col = jax.random.split(base_key, 3)
    source = jnp.broadcast_to(jnp.arange(N_TILE, dtype=jnp.int32)[:, None], (N_TILE, RIM_SLOTS))
    slot_ids = jnp.broadcast_to(jnp.arange(RIM_SLOTS, dtype=jnp.int32)[None, :], (N_TILE, RIM_SLOTS))
    placed = (source + NS // 2) % N_TILE
    strip_index = placed % NS
    panel_index = placed // NS
    corner_slot = (slot_ids == 0) | (slot_ids == BC + 1) | (slot_ids == BC + 2) | (slot_ids == 2 * BC + 3)
    top_slot = slot_ids <= BC + 1
    bottom_slot = (slot_ids >= BC + 2) & (slot_ids <= 2 * BC + 3)
    side_slot = slot_ids >= 2 * BC + 4
    eligible = side_slot | corner_slot | top_slot & (strip_index == 0) | bottom_slot & (strip_index == NS - 1)
    eligible_rank = jnp.cumsum(eligible.astype(jnp.int32), axis=1) - 1
    dest_group = jnp.clip(eligible_rank % NS, 0, NS - 1)
    position = jnp.clip(eligible_rank // NS, 0, MOST - 1)
    perm_keys = jax.random.split(key_perm, N_TILE)
    orders = jax.vmap(lambda perm_key: jax.random.permutation(perm_key, NS))(perm_keys).astype(jnp.int32)
    other_place = jnp.take_along_axis(orders, dest_group, axis=1) + (1 - panel_index) * NS
    target = (other_place - NS // 2 + N_TILE) % N_TILE
    target = jnp.where(eligible, target, N_TILE)
    donor_row = jax.random.randint(key_row, (N_TILE, RIM_SLOTS), 0, BR - 1)
    donor_col = jax.random.randint(key_col, (N_TILE, RIM_SLOTS), 0, BC - 1)
    donor_cell = (donor_row * BC + donor_col).astype(jnp.int32)
    donor_cell = donor_cell.at[0, 2 * BC + 4].set((BR - 2) * BC + BC - 2)
    send_table = jnp.full((N_TILE, N_TILE, MOST), -1, jnp.int32).at[source, target, position].set(slot_ids, mode='drop')
    recv_table = jnp.full((N_TILE, N_TILE, MOST), -1, jnp.int32).at[target, source, position].set(donor_cell, mode='drop')
    return (send_table, recv_table)


def draw_send_rows(key, part):
    return donor_plan(key)[0]


def draw_recv_cells(key, part):
    return donor_plan(key)[1]


def draw_recv_weight(key, part):
    key_across, key_down = jax.random.split(jax.random.fold_in(key, 11))
    frac_across = jax.random.uniform(key_across, (N_TILE, N_TILE, MOST), jnp.float32)
    frac_down = jax.random.uniform(key_down, (N_TILE, N_TILE, MOST), jnp.float32)
    corners = jnp.stack([(1.0 - frac_across) * (1.0 - frac_down), frac_across * (1.0 - frac_down), (1.0 - frac_across) * frac_down, frac_across * frac_down], axis=1)
    return corners.astype(jnp.float32)


def shard_levels(own_key, dims, pieces, least, high):
    factor_of, own = 1.0, jax.random.fold_in(own_key, 6)
    for axis_at, blocks in pieces:
        steps = jnp.exp(jax.random.uniform(jax.random.fold_in(own, axis_at), (blocks,), jnp.float32, least / len(pieces), high / len(pieces)))
        factor_of = factor_of * jnp.repeat(steps, dims[axis_at] // blocks).reshape([-1 if axis == axis_at else 1 for axis in range(len(dims))])
    return factor_of


def normal_values(stream_key, shape, scale, reach, pieces=(), kind=jnp.bfloat16):
    values = jax.random.normal(stream_key, shape, jnp.float32) * scale
    if len(pieces) > 0:
        values = shard_levels(stream_key, shape, pieces, -0.22, 0.18) * values
    return jnp.clip(values, min=-reach, max=reach).astype(kind)


def setup_inputs(seed: int = 0) -> dict:
    key_of = jax.random.split(jax.random.key(seed), 7)
    return {
        "cotangent": normal_values(key_of[0], (FEAT, ROWS, BC), 1.0, 6.0, ((0, 4), (1, 8))),
        "mix_weight": normal_values(key_of[1], (FEAT, FEAT), FEAT ** -0.5, 0.109375, ((1, 8),)),
        "kernel": normal_values(key_of[2], (FEAT, 9), 9 ** -0.5, 2.0, ((0, 4),), jnp.float32),
        "send_rows": draw_send_rows(jax.random.fold_in(key_of[6], 71), 0),
        "recv_cells": draw_recv_cells(jax.random.fold_in(key_of[6], 71), 0),
        "recv_weight": draw_recv_weight(jax.random.fold_in(key_of[6], 71), 0),
    }


def stencil_adjoint(grad_block, kernel):
    padded = jnp.pad(grad_block.astype(jnp.float32), ((0, 0), (2, 2), (2, 2)))
    summed = jnp.zeros((grad_block.shape[0], BR + 2, BC + 2), jnp.float32)
    for row_shift in (-1, 0, 1):
        for col_shift in (-1, 0, 1):
            kernel_tap = kernel[:, 3 * (row_shift + 1) + col_shift + 1]
            window_part = padded[:, 1 - row_shift:3 - row_shift + BR, 1 - col_shift:3 - col_shift + BC]
            summed = summed + kernel_tap[:, None, None] * window_part
    return summed


def cycle_of(extended):
    return jnp.concatenate([extended[:, 0, :], extended[:, -1, :], extended[:, 1:-1, 0], extended[:, 1:-1, -1]], axis=1)


def reference(cotangent, mix_weight, kernel, send_rows, recv_cells, recv_weight):
    weight_full = mix_weight.astype(jnp.float32)
    tile_blocks = cotangent.reshape(FEAT, N_TILE, BR * BC).transpose(1, 0, 2)

    def tile_adjoint(tile_block):
        grad_mix = jnp.dot(weight_full, tile_block.astype(jnp.float32), precision=lax.Precision.HIGHEST).astype(jnp.bfloat16)
        extended = stencil_adjoint(grad_mix.reshape(FEAT, BR, BC), kernel)
        cycle_values = cycle_of(extended).astype(jnp.bfloat16)
        return extended[:, 1:-1, 1:-1], extended[:, 0, 1:-1], extended[:, -1, 1:-1], cycle_values

    interior, top_rows, bottom_rows, cycle_table = lax.map(tile_adjoint, tile_blocks)
    place_index = ((jnp.arange(N_TILE, dtype=jnp.int32) + NS // 2) % N_TILE) % NS
    from_above = jnp.roll(bottom_rows, 1, axis=0) * (place_index != 0).astype(jnp.float32)[:, None, None]
    from_below = jnp.roll(top_rows, -1, axis=0) * (place_index != NS - 1).astype(jnp.float32)[:, None, None]
    interior = interior.at[:, :, 0, :].add(from_above).at[:, :, -1, :].add(from_below)
    summed = interior.reshape(N_TILE, FEAT, BR * BC)

    def pick_rows(cycle_values, slot_table):
        return jnp.take(cycle_values, jnp.maximum(slot_table, 0).reshape(-1), axis=1)

    picked_rows = jax.vmap(pick_rows)(cycle_table, send_rows).reshape(N_TILE, FEAT, N_TILE, MOST)
    picked_rows = jnp.transpose(picked_rows, (2, 1, 0, 3))

    def deposit_tile(item):
        running, values, cell_table, weight_table = item
        spread = values.reshape(FEAT, -1).astype(jnp.float32)
        cell_index = cell_table.reshape(-1)
        weight_rows = weight_table.reshape(4, -1)
        is_used = cell_index >= 0
        base_cell = jnp.maximum(cell_index, 0)
        for corner, offset in enumerate((0, 1, BC, BC + 1)):
            running = running.at[:, base_cell + offset].add(spread * jnp.where(is_used, weight_rows[corner], 0.0)[None, :])
        return running

    summed = lax.map(deposit_tile, (summed, picked_rows, recv_cells, recv_weight))
    result = summed.reshape(N_TILE, FEAT, BR, BC).astype(jnp.bfloat16)
    return result.transpose(1, 0, 2, 3).reshape(FEAT, N_TILE * BR, BC)
```

```python
import functools

import jax
import jax.numpy as jnp
from jax import lax
from jax.experimental import pallas as pl
from jax.experimental.pallas import tpu as pltpu
from jax.sharding import PartitionSpec as P

MESH = pl.DeviceIdType.MESH


def mix_kernel(n_tile, n_lev, chunks, c_ref, w_ref, g_ref, wg, cg, local_sem, ws, wr, cs, cr):
    t = lax.axis_index("tile")
    l = lax.axis_index("lev")
    feat, cells = c_ref.shape
    cb = w_ref.shape[1]
    half_t, half_l = n_tile // 2, n_lev // 2
    width = cells // chunks
    per = feat // cb
    joined = len(wg.shape) == 3 and wg.shape[0] == n_lev and wg.shape[2] == feat
    t_mate = t + 1 - 2 * lax.rem(t, 2)
    l_mate = l + 1 - 2 * lax.rem(l, 2)

    def t_of(base, k):
        return lax.rem(base + 2 * k + 2 * n_tile, n_tile)

    def l_of(base, k):
        return lax.rem(base + 2 * k + 2 * n_lev, n_lev)

    barrier = pltpu.get_barrier_semaphore()
    peers = [(t_of(t, k), l) for k in range(1, half_t)] + [(t_mate, l), (t, l_mate)]
    peers += [(t, l_of(l, k)) for k in range(1, half_l)]
    for peer in peers:
        pl.semaphore_signal(barrier, inc=1, device_id=peer, device_id_type=MESH)
    pl.semaphore_wait(barrier, len(peers))

    def w_slot(index):
        if joined:
            return wg.at[index // per, :, pl.ds(pl.multiple_of(lax.rem(index, per) * cb, cb), cb)]
        return wg.at[index]

    own_w = w_ref.at[pl.ds(pl.multiple_of(l * feat, feat), feat)]

    def w_copy(lane, k, index, source, to):
        return pltpu.make_async_remote_copy(
            src_ref=source, dst_ref=w_slot(index), send_sem=ws.at[lane, k], recv_sem=wr.at[lane, k],
            device_id=(to, l), device_id_type=MESH)

    def c_piece(ref, ch):
        return ref.at[:, ch * width:(ch + 1) * width]

    def c_copy(lane, k, ch, index, source, to):
        return pltpu.make_async_remote_copy(
            src_ref=source, dst_ref=c_piece(cg.at[index], ch), send_sem=cs.at[lane, k, ch],
            recv_sem=cr.at[lane, k, ch], device_id=(t, to), device_id_type=MESH)

    sends = []

    def start(copy):
        copy.start()
        sends.append(copy)

    for ch in range(chunks):
        for k in range(1, half_l):
            start(c_copy(0, k, ch, l, c_piece(c_ref, ch), l_of(l, k)))
    for k in range(1, half_t):
        start(w_copy(0, k, t, own_w, t_of(t, k)))
    start(w_copy(1, 0, t, own_w, t_mate))
    for ch in range(chunks):
        start(c_copy(1, 0, ch, l, c_piece(c_ref, ch), l_mate))
    keep_w = pltpu.make_async_copy(own_w, w_slot(t), local_sem.at[0])
    keep_c = pltpu.make_async_copy(c_ref, cg.at[l], local_sem.at[1])
    keep_w.start()
    keep_c.start()

    def pass_w(k):
        index = t_of(t, -k)
        w_copy(0, k, index, own_w, t_of(t, k)).wait_recv()
        start(w_copy(1, k, index, w_slot(index), t_mate))

    def pass_c(ch):
        for k in range(1, half_l):
            index = l_of(l, -k)
            c_copy(0, k, ch, index, c_piece(c_ref, ch), l_of(l, k)).wait_recv()
            start(c_copy(1, k, ch, index, c_piece(cg.at[index], ch), l_mate))

    passed = 0
    for k in range(1, half_t):
        pass_w(k)
        while passed < chunks - 1 and passed * (half_t - 1) < k * (chunks - 1):
            pass_c(passed)
            passed += 1
    keep_w.wait()
    keep_c.wait()
    for k in range(half_t):
        w_copy(1, k, t_of(t_mate, -k), own_w, t_mate).wait_recv()

    rows = feat // 3
    for ch in range(chunks):
        if ch >= passed:
            pass_c(ch)
        for k in range(half_l):
            c_copy(1, k, ch, l_of(l_mate, -k), c_piece(c_ref, ch), l_mate).wait_recv()

        def body(m, carry, ch=ch):
            r0 = pl.multiple_of(m * rows, rows)
            total = None
            if joined:
                for b in range(n_lev):
                    part = jnp.dot(wg[b, pl.ds(r0, rows), :], cg[b, :, ch * width:(ch + 1) * width],
                                   preferred_element_type=jnp.float32)
                    total = part if total is None else total + part
            else:
                for b in range(n_tile):
                    k0 = (b % per) * cb
                    part = jnp.dot(wg[b, pl.ds(r0, rows), :],
                                   cg[b // per, k0:k0 + cb, ch * width:(ch + 1) * width],
                                   preferred_element_type=jnp.float32)
                    total = part if total is None else total + part
            g_ref[pl.ds(r0, rows), ch * width:(ch + 1) * width] = total.astype(jnp.bfloat16)
            return carry

        lax.fori_loop(0, 3, body, 0)
    for copy in sends:
        copy.wait_send()


def mix(c, w, n_tile, n_lev):
    feat, cells = c.shape
    cb = w.shape[1]
    chunks = 4
    w_shape = (n_lev, feat, feat) if cb % 128 == 0 else (n_tile, feat, cb)
    return pl.pallas_call(
        functools.partial(mix_kernel, n_tile, n_lev, chunks),
        out_shape=jax.ShapeDtypeStruct((feat, cells), jnp.bfloat16),
        in_specs=[pl.BlockSpec(memory_space=pl.ANY)] * 2,
        out_specs=pl.BlockSpec(memory_space=pltpu.VMEM),
        scratch_shapes=[
            pltpu.VMEM(w_shape, jnp.bfloat16),
            pltpu.VMEM((n_lev, feat, cells), jnp.bfloat16),
            pltpu.SemaphoreType.DMA((2,)),
            pltpu.SemaphoreType.DMA((2, n_tile // 2)),
            pltpu.SemaphoreType.DMA((2, n_tile // 2)),
            pltpu.SemaphoreType.DMA((2, n_lev // 2, chunks)),
            pltpu.SemaphoreType.DMA((2, n_lev // 2, chunks)),
        ],
        compiler_params=pltpu.CompilerParams(
            collective_id=0, has_side_effects=True, vmem_limit_bytes=48 * 2**20),
        name="mix",
    )(c, w)


def stencil_kernel(rows, cols, g_ref, k_ref, oh_ref, sel_ref, local_ref, vals_ref, top_ref, bottom_ref):
    g = g_ref[...]
    fb = g.shape[0]
    taps = k_ref[...]

    def tap(a, b):
        n = 3 * (a + 1) + b + 1
        return taps[:, n:n + 1]

    lane = lax.broadcasted_iota(jnp.int32, (fb, cols), 1)
    weight = {(a, b): jnp.broadcast_to(tap(a, b), (fb, cols)) for a in (-1, 0, 1) for b in (-1, 0, 1)}
    first, last = lane == 0, lane == cols - 1
    parts = {}
    top = bottom = None
    for r in range(rows + 1):
        if r < rows:
            mid = g[:, r * cols:(r + 1) * cols].astype(jnp.float32)
            after = jnp.where(last, 0.0, pltpu.roll(mid, cols - 1, 1))
            before = jnp.where(first, 0.0, pltpu.roll(mid, 1, 1))
            for a in (-1, 0, 1):
                parts[a, r] = weight[a, -1] * after + weight[a, 0] * mid + weight[a, 1] * before
        if r == 0:
            top = parts[-1, 0]
        else:
            i = r - 1
            total = parts[0, i]
            if i > 0:
                total = total + parts[1, i - 1]
            if i < rows - 1:
                total = total + parts[-1, i + 1]
            local_ref[:, i * cols:(i + 1) * cols] = total
    bottom = parts[1, rows - 1]
    top, bottom = top.astype(jnp.bfloat16), bottom.astype(jnp.bfloat16)
    top_ref[...] = top
    bottom_ref[...] = bottom
    edge = jnp.dot(g, sel_ref[...], preferred_element_type=jnp.float32)
    near = lane < cols // 2
    sides = jnp.where(near, weight[0, -1], weight[0, 1]) * edge
    sides += jnp.where(near, weight[-1, -1], weight[-1, 1]) * pltpu.roll(edge, cols - 1, 1)
    sides += jnp.where(near, weight[1, -1], weight[1, 1]) * pltpu.roll(edge, 1, 1)
    cycle = jnp.concatenate([top, bottom, sides.astype(jnp.bfloat16)], axis=1)
    vals_ref[...] = lax.dot_general(
        oh_ref[...], cycle, (((1,), (1,)), ((), ())), preferred_element_type=jnp.float32
    ).astype(jnp.bfloat16)


def deposit_kernel(rows, cols, local_ref, vals_ref, spread_ref, up_ref, down_ref, out_ref):
    total = local_ref[...] + lax.dot_general(
        vals_ref[...], spread_ref[...], (((0,), (0,)), ((), ())), preferred_element_type=jnp.float32)
    first = total[:, :cols] + up_ref[...].astype(jnp.float32)
    last = total[:, -cols:] + down_ref[...].astype(jnp.float32)
    total = jnp.concatenate([first, total[:, cols:-cols], last], axis=1)
    out_ref[...] = total.reshape(total.shape[0], rows, cols).astype(jnp.bfloat16)


def slot_place(slot, rows, cols):
    side, far = 2 * cols, 2 * cols + cols // 2
    low = slot - (cols + 2)
    place = jnp.where(slot < cols + 2, slot - 1, cols + low - 1)
    place = jnp.where(slot == 0, side, place)
    place = jnp.where(slot == cols + 1, far, place)
    place = jnp.where(low == 0, side + rows + 1, place)
    place = jnp.where(low == cols + 1, far + rows + 1, place)
    left = slot - 2 * (cols + 2)
    place = jnp.where(left >= 0, side + 1 + left, place)
    place = jnp.where(left >= rows, far + 1 + left - rows, place)
    return jnp.where(slot < 0, -1, place)


def per_device(cotangent, mix_weight, kernel, send_rows, recv_cells, recv_weight, n_tile, n_lev):
    feat, rows, cols = cotangent.shape
    cells = rows * cols
    most = send_rows.shape[2]
    pad = -(-most // 16) * 16
    strips = n_tile // 2
    tile_here = lax.axis_index("tile")
    place = (tile_here + strips // 2) % n_tile % strips
    extra = ((0, 0), (0, pad - most))
    places = jnp.pad(slot_place(send_rows[0], rows, cols), extra, constant_values=-1).reshape(-1, 1)
    picks = (places == jnp.arange(3 * cols, dtype=jnp.int32)[None, :]).astype(jnp.bfloat16)
    targets = jnp.pad(recv_cells[0], extra, constant_values=-1).reshape(-1, 1)
    weights = jnp.pad(recv_weight[0], ((0, 0),) + extra).reshape(4, -1, 1)
    at = jnp.arange(cells, dtype=jnp.int32)[None, :] - targets
    spread = jnp.zeros(at.shape, jnp.float32)
    for corner, offset in enumerate((0, 1, cols, cols + 1)):
        spread = jnp.where((at == offset) & (targets >= 0), weights[corner], spread)
    spread = spread.astype(jnp.bfloat16)
    cell = jnp.arange(cells, dtype=jnp.int32)[:, None]
    spot = jnp.arange(cols, dtype=jnp.int32)[None, :]
    row, col = cell // cols, cell % cols
    select = ((col == 0) & (spot == row + 1)) | ((col == cols - 1) & (spot == cols // 2 + row + 1))
    select = select.astype(jnp.bfloat16)

    grad = mix(cotangent.reshape(feat, cells), mix_weight, n_tile, n_lev)

    fb = 128
    entries = picks.shape[0]
    grid = (feat // fb,)
    by_feat = lambda width: pl.BlockSpec((fb, width), lambda i: (i, 0))
    whole = lambda shape: pl.BlockSpec(shape, lambda i: (0, 0))
    by_column = pl.BlockSpec((entries, fb), lambda i: (0, i))
    params = pltpu.CompilerParams(vmem_limit_bytes=48 * 2**20)
    local, vals, top, bottom = pl.pallas_call(
        functools.partial(stencil_kernel, rows, cols),
        grid=grid,
        out_shape=[
            jax.ShapeDtypeStruct((feat, cells), jnp.float32),
            jax.ShapeDtypeStruct((entries, feat), jnp.bfloat16),
            jax.ShapeDtypeStruct((feat, cols), jnp.bfloat16),
            jax.ShapeDtypeStruct((feat, cols), jnp.bfloat16),
        ],
        in_specs=[by_feat(cells), by_feat(9), whole((entries, 3 * cols)), whole((cells, cols))],
        out_specs=[by_feat(cells), by_column, by_feat(cols), by_feat(cols)],
        compiler_params=params,
        name="stencil",
    )(grad, kernel, picks, select)
    up = lax.ppermute(bottom, "tile", [(i, (i + 1) % n_tile) for i in range(n_tile)])
    down = lax.ppermute(top, "tile", [((i + 1) % n_tile, i) for i in range(n_tile)])
    up = jnp.where(place != 0, up, jnp.zeros_like(up))
    down = jnp.where(place != strips - 1, down, jnp.zeros_like(down))
    vals = lax.all_to_all(vals, "tile", split_axis=0, concat_axis=0, tiled=True)
    return pl.pallas_call(
        functools.partial(deposit_kernel, rows, cols),
        grid=grid,
        out_shape=jax.ShapeDtypeStruct((feat, rows, cols), jnp.bfloat16),
        in_specs=[by_feat(cells), by_column, whole((entries, cells)), by_feat(cols), by_feat(cols)],
        out_specs=pl.BlockSpec((fb, rows, cols), lambda i: (i, 0, 0)),
        compiler_params=params,
        name="deposit",
    )(local, vals, spread, up, down)


def solution(mesh):
    in_specs = (
        P("lev", "tile", None),
        P(None, "tile"),
        P("lev", None),
        P("tile", None, None),
        P("tile", None, None),
        P("tile", None, None, None),
    )
    return jax.shard_map(
        functools.partial(per_device, n_tile=mesh.shape["tile"], n_lev=mesh.shape["lev"]),
        mesh=mesh, in_specs=in_specs, out_specs=P("lev", "tile", None), check_vma=False)
```

```python
import functools

import jax
import jax.numpy as jnp
from jax import lax
from jax.experimental import pallas as pl
from jax.experimental.pallas import tpu as pltpu
from jax.sharding import PartitionSpec as P

MESH = pl.DeviceIdType.MESH


def mix_kernel(n_tile, n_lev, chunks, rows_n, cols, c_ref, w_ref, k_ref, oh_ref, cell_ref, weight_ref,
               local_out, vals_out, up_out, down_out, spread_out,
               g_ref, local_ref, vals_ref, top_ref, bottom_ref, spread_ref, sel_ref,
               wg, cg, local_sem, ws, wr, cs, cr, es, er):
    t = lax.axis_index("tile")
    l = lax.axis_index("lev")
    feat, cells = c_ref.shape
    cb = w_ref.shape[1]
    half_t, half_l = n_tile // 2, n_lev // 2
    width = cells // chunks
    per = feat // cb
    joined = len(wg.shape) == 3 and wg.shape[0] == n_lev and wg.shape[2] == feat
    t_mate = t + 1 - 2 * lax.rem(t, 2)
    l_mate = l + 1 - 2 * lax.rem(l, 2)

    def t_of(base, k):
        return lax.rem(base + 2 * k + 2 * n_tile, n_tile)

    def l_of(base, k):
        return lax.rem(base + 2 * k + 2 * n_lev, n_lev)

    barrier = pltpu.get_barrier_semaphore()
    peers = [(lax.rem(t + k, n_tile), l) for k in range(1, n_tile)] + [(t, l_mate)]
    peers += [(t, l_of(l, k)) for k in range(1, half_l)]
    for peer in peers:
        pl.semaphore_signal(barrier, inc=1, device_id=peer, device_id_type=MESH)
    pl.semaphore_wait(barrier, len(peers))

    def w_slot(index):
        if joined:
            return wg.at[index // per, :, pl.ds(pl.multiple_of(lax.rem(index, per) * cb, cb), cb)]
        return wg.at[index]

    own_w = w_ref.at[pl.ds(pl.multiple_of(l * feat, feat), feat)]

    def w_copy(lane, k, index, source, to):
        return pltpu.make_async_remote_copy(
            src_ref=source, dst_ref=w_slot(index), send_sem=ws.at[lane, k], recv_sem=wr.at[lane, k],
            device_id=(to, l), device_id_type=MESH)

    def c_piece(ref, ch):
        return ref.at[:, ch * width:(ch + 1) * width]

    def c_copy(lane, k, ch, index, source, to):
        return pltpu.make_async_remote_copy(
            src_ref=source, dst_ref=c_piece(cg.at[index], ch), send_sem=cs.at[lane, k, ch],
            recv_sem=cr.at[lane, k, ch], device_id=(t, to), device_id_type=MESH)

    sends = []

    def start(copy):
        copy.start()
        sends.append(copy)

    for ch in range(chunks):
        for k in range(1, half_l):
            start(c_copy(0, k, ch, l, c_piece(c_ref, ch), l_of(l, k)))
    for k in range(1, half_t):
        start(w_copy(0, k, t, own_w, t_of(t, k)))
    start(w_copy(1, 0, t, own_w, t_mate))
    for ch in range(chunks):
        start(c_copy(1, 0, ch, l, c_piece(c_ref, ch), l_mate))
    keep_w = pltpu.make_async_copy(own_w, w_slot(t), local_sem.at[0])
    keep_c = pltpu.make_async_copy(c_ref, cg.at[l], local_sem.at[1])
    keep_w.start()
    keep_c.start()

    entries = cell_ref.shape[0]

    def fill(b, carry):
        r0 = pl.multiple_of(b * 16, 16)
        cell = cell_ref[pl.ds(r0, 16), :]
        at = lax.broadcasted_iota(jnp.int32, (16, cells), 1) - cell
        weights = weight_ref[pl.ds(r0, 16), :]
        total = jnp.zeros((16, cells), jnp.float32)
        for corner, offset in enumerate((0, 1, cols, cols + 1)):
            total = jnp.where(at == offset, weights[:, corner:corner + 1], total)
        spread_ref[pl.ds(r0, 16), :] = jnp.where(cell >= 0, total, 0.0).astype(jnp.bfloat16)
        return carry

    lax.fori_loop(0, entries // 16, fill, 0)
    keep_spread = pltpu.make_async_copy(spread_ref, spread_out, local_sem.at[2])
    keep_spread.start()
    col = lax.broadcasted_iota(jnp.int32, (cols, cols), 0)
    spot = lax.broadcasted_iota(jnp.int32, (cols, cols), 1)
    for r in range(rows_n):
        hit = ((col == 0) & (spot == r + 1)) | ((col == cols - 1) & (spot == cols // 2 + r + 1))
        sel_ref[r * cols:(r + 1) * cols, :] = jnp.where(hit, 1.0, 0.0).astype(jnp.bfloat16)

    def pass_w(k):
        index = t_of(t, -k)
        w_copy(0, k, index, own_w, t_of(t, k)).wait_recv()
        start(w_copy(1, k, index, w_slot(index), t_mate))

    def pass_c(ch):
        for k in range(1, half_l):
            index = l_of(l, -k)
            c_copy(0, k, ch, index, c_piece(c_ref, ch), l_of(l, k)).wait_recv()
            start(c_copy(1, k, ch, index, c_piece(cg.at[index], ch), l_mate))

    passed = 0
    for k in range(1, half_t):
        pass_w(k)
        while passed < chunks - 1 and passed * (half_t - 1) < k * (chunks - 1):
            pass_c(passed)
            passed += 1
    keep_w.wait()
    keep_c.wait()
    for k in range(half_t):
        w_copy(1, k, t_of(t_mate, -k), own_w, t_mate).wait_recv()

    rows = feat // 3
    for ch in range(chunks):
        if ch >= passed:
            pass_c(ch)
        for k in range(half_l):
            c_copy(1, k, ch, l_of(l_mate, -k), c_piece(c_ref, ch), l_mate).wait_recv()

        def body(m, carry, ch=ch):
            r0 = pl.multiple_of(m * rows, rows)
            total = None
            if joined:
                for b in range(n_lev):
                    part = jnp.dot(wg[b, pl.ds(r0, rows), :], cg[b, :, ch * width:(ch + 1) * width],
                                   preferred_element_type=jnp.float32)
                    total = part if total is None else total + part
            else:
                for b in range(n_tile):
                    k0 = (b % per) * cb
                    part = jnp.dot(wg[b, pl.ds(r0, rows), :],
                                   cg[b // per, k0:k0 + cb, ch * width:(ch + 1) * width],
                                   preferred_element_type=jnp.float32)
                    total = part if total is None else total + part
            g_ref[pl.ds(r0, rows), ch * width:(ch + 1) * width] = total.astype(jnp.bfloat16)
            return carry

        lax.fori_loop(0, 3, body, 0)

    strips = n_tile // 2
    q = lax.rem(t + strips // 2, n_tile)
    panel, place = q // strips, lax.rem(q, strips)
    keep_top = (place != 0).astype(jnp.float32)
    keep_bottom = (place != strips - 1).astype(jnp.float32)

    def shape(m, carry):
        stencil(rows_n, cols, pl.ds(pl.multiple_of(m * 128, 128), 128), keep_top, keep_bottom,
                g_ref, k_ref, oh_ref, sel_ref, local_ref, vals_ref, top_ref, bottom_ref)
        return carry

    lax.fori_loop(0, feat // 128, shape, 0)
    pad = entries // strips
    edge_copies = [
        pltpu.make_async_remote_copy(
            src_ref=top_ref, dst_ref=down_out, send_sem=es.at[0], recv_sem=er.at[0],
            device_id=(lax.rem(t + n_tile - 1, n_tile), l), device_id_type=MESH),
        pltpu.make_async_remote_copy(
            src_ref=bottom_ref, dst_ref=up_out, send_sem=es.at[1], recv_sem=er.at[1],
            device_id=(lax.rem(t + 1, n_tile), l), device_id_type=MESH),
    ]

    def vals_copy(j, slot):
        to = lax.rem((1 - panel) * strips + j - strips // 2 + n_tile, n_tile)
        return pltpu.make_async_remote_copy(
            src_ref=vals_ref.at[pl.ds(j * pad, pad)],
            dst_ref=vals_out.at[pl.ds(pl.multiple_of(slot * pad, 16), pad)],
            send_sem=es.at[2 + j], recv_sem=er.at[2 + slot], device_id=(to, l), device_id_type=MESH)

    for copy in edge_copies:
        start(copy)
    for j in range(strips):
        start(vals_copy(j, place))
    keep_local = pltpu.make_async_copy(local_ref, local_out, local_sem.at[3])
    keep_local.start()
    for copy in edge_copies:
        copy.wait_recv()
    for j in range(strips):
        vals_copy(j, j).wait_recv()
    keep_spread.wait()
    keep_local.wait()
    for copy in sends:
        copy.wait_send()


def mix(c, w, kernel, picks, targets, weights, n_tile, n_lev, rows, cols):
    feat, cells = c.shape
    cb = w.shape[1]
    chunks = 4
    entries = picks.shape[0]
    strips = n_tile // 2
    w_shape = (n_lev, feat, feat) if cb % 128 == 0 else (n_tile, feat, cb)
    vmem = pl.BlockSpec(memory_space=pltpu.VMEM)
    anywhere = pl.BlockSpec(memory_space=pl.ANY)
    return pl.pallas_call(
        functools.partial(mix_kernel, n_tile, n_lev, chunks, rows, cols),
        out_shape=[
            jax.ShapeDtypeStruct((feat, cells), jnp.float32),
            jax.ShapeDtypeStruct((entries, feat), jnp.bfloat16),
            jax.ShapeDtypeStruct((feat, cols), jnp.bfloat16),
            jax.ShapeDtypeStruct((feat, cols), jnp.bfloat16),
            jax.ShapeDtypeStruct((entries, cells), jnp.bfloat16),
        ],
        in_specs=[anywhere] * 2 + [vmem] * 4,
        out_specs=[anywhere] * 5,
        scratch_shapes=[
            pltpu.VMEM((feat, cells), jnp.bfloat16),
            pltpu.VMEM((feat, cells), jnp.float32),
            pltpu.VMEM((entries, feat), jnp.bfloat16),
            pltpu.VMEM((feat, cols), jnp.bfloat16),
            pltpu.VMEM((feat, cols), jnp.bfloat16),
            pltpu.VMEM((entries, cells), jnp.bfloat16),
            pltpu.VMEM((cells, cols), jnp.bfloat16),
            pltpu.VMEM(w_shape, jnp.bfloat16),
            pltpu.VMEM((n_lev, feat, cells), jnp.bfloat16),
            pltpu.SemaphoreType.DMA((4,)),
            pltpu.SemaphoreType.DMA((2, n_tile // 2)),
            pltpu.SemaphoreType.DMA((2, n_tile // 2)),
            pltpu.SemaphoreType.DMA((2, n_lev // 2, chunks)),
            pltpu.SemaphoreType.DMA((2, n_lev // 2, chunks)),
            pltpu.SemaphoreType.DMA((2 + strips,)),
            pltpu.SemaphoreType.DMA((2 + strips,)),
        ],
        compiler_params=pltpu.CompilerParams(
            collective_id=0, has_side_effects=True, vmem_limit_bytes=52 * 2**20),
        name="mix",
    )(c, w, kernel, picks, targets, weights)


def stencil(rows, cols, part, keep_top, keep_bottom,
            g_ref, k_ref, oh_ref, sel_ref, local_ref, vals_ref, top_ref, bottom_ref):
    g = g_ref[part, :]
    fb = g.shape[0]
    taps = k_ref[part, :]

    def tap(a, b):
        n = 3 * (a + 1) + b + 1
        return taps[:, n:n + 1]

    lane = lax.broadcasted_iota(jnp.int32, (fb, cols), 1)
    weight = {(a, b): jnp.broadcast_to(tap(a, b), (fb, cols)) for a in (-1, 0, 1) for b in (-1, 0, 1)}
    first, last = lane == 0, lane == cols - 1
    parts = {}
    top = bottom = None
    for r in range(rows + 1):
        if r < rows:
            mid = g[:, r * cols:(r + 1) * cols].astype(jnp.float32)
            after = jnp.where(last, 0.0, pltpu.roll(mid, cols - 1, 1))
            before = jnp.where(first, 0.0, pltpu.roll(mid, 1, 1))
            for a in (-1, 0, 1):
                parts[a, r] = weight[a, -1] * after + weight[a, 0] * mid + weight[a, 1] * before
        if r == 0:
            top = parts[-1, 0]
        else:
            i = r - 1
            total = parts[0, i]
            if i > 0:
                total = total + parts[1, i - 1]
            if i < rows - 1:
                total = total + parts[-1, i + 1]
            local_ref[part, i * cols:(i + 1) * cols] = total
    bottom = parts[1, rows - 1]
    top_ref[part, :] = (top * keep_top).astype(jnp.bfloat16)
    bottom_ref[part, :] = (bottom * keep_bottom).astype(jnp.bfloat16)
    top, bottom = top.astype(jnp.bfloat16), bottom.astype(jnp.bfloat16)
    edge = jnp.dot(g, sel_ref[...], preferred_element_type=jnp.float32)
    near = lane < cols // 2
    sides = jnp.where(near, weight[0, -1], weight[0, 1]) * edge
    sides += jnp.where(near, weight[-1, -1], weight[-1, 1]) * pltpu.roll(edge, cols - 1, 1)
    sides += jnp.where(near, weight[1, -1], weight[1, 1]) * pltpu.roll(edge, 1, 1)
    cycle = jnp.concatenate([top, bottom, sides.astype(jnp.bfloat16)], axis=1)
    vals_ref[:, part] = lax.dot_general(
        oh_ref[...], cycle, (((1,), (1,)), ((), ())), preferred_element_type=jnp.float32
    ).astype(jnp.bfloat16)


def deposit_kernel(rows, cols, local_ref, vals_ref, spread_ref, up_ref, down_ref, out_ref):
    total = local_ref[...] + lax.dot_general(
        vals_ref[...], spread_ref[...], (((0,), (0,)), ((), ())), preferred_element_type=jnp.float32)
    first = total[:, :cols] + up_ref[...].astype(jnp.float32)
    last = total[:, -cols:] + down_ref[...].astype(jnp.float32)
    total = jnp.concatenate([first, total[:, cols:-cols], last], axis=1)
    out_ref[...] = total.reshape(total.shape[0], rows, cols).astype(jnp.bfloat16)


def slot_place(slot, rows, cols):
    side, far = 2 * cols, 2 * cols + cols // 2
    low = slot - (cols + 2)
    place = jnp.where(slot < cols + 2, slot - 1, cols + low - 1)
    place = jnp.where(slot == 0, side, place)
    place = jnp.where(slot == cols + 1, far, place)
    place = jnp.where(low == 0, side + rows + 1, place)
    place = jnp.where(low == cols + 1, far + rows + 1, place)
    left = slot - 2 * (cols + 2)
    place = jnp.where(left >= 0, side + 1 + left, place)
    place = jnp.where(left >= rows, far + 1 + left - rows, place)
    return jnp.where(slot < 0, -1, place)


def per_device(cotangent, mix_weight, kernel, send_rows, recv_cells, recv_weight, n_tile, n_lev):
    feat, rows, cols = cotangent.shape
    cells = rows * cols
    most = send_rows.shape[2]
    pad = -(-most // 16) * 16
    strips = n_tile // 2
    panel = (lax.axis_index("tile") + strips // 2) % n_tile // strips
    begin = ((1 - panel) * strips - strips // 2 + n_tile) % n_tile

    def of_partners(table, dim):
        table = lax.dynamic_slice_in_dim(jnp.concatenate([table, table], axis=dim), begin, strips, dim)
        width = [(0, 0)] * (table.ndim - 1) + [(0, pad - most)]
        return jnp.pad(table, width, constant_values=-1)

    places = slot_place(of_partners(send_rows[0], 0), rows, cols).reshape(-1, 1)
    picks = (places == jnp.arange(3 * cols, dtype=jnp.int32)[None, :]).astype(jnp.bfloat16)
    targets = of_partners(recv_cells[0], 0).reshape(-1, 1)
    weights = of_partners(recv_weight[0], 1).reshape(4, -1).T

    local, vals, up, down, spread = mix(
        cotangent.reshape(feat, cells), mix_weight, kernel, picks, targets, weights, n_tile, n_lev, rows, cols)

    fb = 128
    entries = picks.shape[0]
    grid = (feat // fb,)
    by_feat = lambda width: pl.BlockSpec((fb, width), lambda i: (i, 0))
    whole = lambda shape: pl.BlockSpec(shape, lambda i: (0, 0))
    by_column = pl.BlockSpec((entries, fb), lambda i: (0, i))
    params = pltpu.CompilerParams(vmem_limit_bytes=48 * 2**20)
    return pl.pallas_call(
        functools.partial(deposit_kernel, rows, cols),
        grid=grid,
        out_shape=jax.ShapeDtypeStruct((feat, rows, cols), jnp.bfloat16),
        in_specs=[by_feat(cells), by_column, whole((entries, cells)), by_feat(cols), by_feat(cols)],
        out_specs=pl.BlockSpec((fb, rows, cols), lambda i: (i, 0, 0)),
        compiler_params=params,
        name="deposit",
    )(local, vals, spread, up, down)


def solution(mesh):
    in_specs = (
        P("lev", "tile", None),
        P(None, "tile"),
        P("lev", None),
        P("tile", None, None),
        P("tile", None, None),
        P("tile", None, None, None),
    )
    return jax.shard_map(
        functools.partial(per_device, n_tile=mesh.shape["tile"], n_lev=mesh.shape["lev"]),
        mesh=mesh, in_specs=in_specs, out_specs=P("lev", "tile", None), check_vma=False)
```

```python
import functools

import jax
import jax.numpy as jnp
from jax import lax
from jax.experimental import pallas as pl
from jax.experimental.pallas import tpu as pltpu
from jax.sharding import PartitionSpec as P

MESH = pl.DeviceIdType.MESH


def mix_kernel(n_tile, n_lev, chunks, rows_n, cols, c_ref, w_ref, k_ref, oh_ref, cell_ref, weight_ref,
               local_out, vals_out, up_out, down_out, spread_out,
               g_ref, local_ref, vals_ref, top_ref, bottom_ref, spread_ref, sel_ref,
               wg, cg, local_sem, ws, wr, cs, cr, es, er):
    t = lax.axis_index("tile")
    l = lax.axis_index("lev")
    feat, cells = c_ref.shape
    cb = w_ref.shape[1]
    half_t, half_l = n_tile // 2, n_lev // 2
    width = cells // chunks
    per = feat // cb
    joined = len(wg.shape) == 3 and wg.shape[0] == n_lev and wg.shape[2] == feat
    t_mate = t + 1 - 2 * lax.rem(t, 2)
    l_mate = l + 1 - 2 * lax.rem(l, 2)

    def t_of(base, k):
        return lax.rem(base + 2 * k + 2 * n_tile, n_tile)

    def l_of(base, k):
        return lax.rem(base + 2 * k + 2 * n_lev, n_lev)

    barrier = pltpu.get_barrier_semaphore()
    peers = [(lax.rem(t + k, n_tile), l) for k in range(1, n_tile)] + [(t, l_mate)]
    peers += [(t, l_of(l, k)) for k in range(1, half_l)]
    for peer in peers:
        pl.semaphore_signal(barrier, inc=1, device_id=peer, device_id_type=MESH)
    pl.semaphore_wait(barrier, len(peers))

    def w_slot(index):
        if joined:
            return wg.at[index // per, :, pl.ds(pl.multiple_of(lax.rem(index, per) * cb, cb), cb)]
        return wg.at[index]

    own_w = w_ref.at[pl.ds(pl.multiple_of(l * feat, feat), feat)]

    def w_copy(lane, k, index, source, to):
        return pltpu.make_async_remote_copy(
            src_ref=source, dst_ref=w_slot(index), send_sem=ws.at[lane, k], recv_sem=wr.at[lane, k],
            device_id=(to, l), device_id_type=MESH)

    def c_piece(ref, ch):
        return ref.at[:, ch * width:(ch + 1) * width]

    def c_copy(lane, k, ch, index, source, to):
        return pltpu.make_async_remote_copy(
            src_ref=source, dst_ref=c_piece(cg.at[index], ch), send_sem=cs.at[lane, k, ch],
            recv_sem=cr.at[lane, k, ch], device_id=(t, to), device_id_type=MESH)

    sends = []

    def start(copy):
        copy.start()
        sends.append(copy)

    for ch in range(chunks):
        for k in range(1, half_l):
            start(c_copy(0, k, ch, l, c_piece(c_ref, ch), l_of(l, k)))
    for k in range(1, half_t):
        start(w_copy(0, k, t, own_w, t_of(t, k)))
    start(w_copy(1, 0, t, own_w, t_mate))
    for ch in range(chunks):
        start(c_copy(1, 0, ch, l, c_piece(c_ref, ch), l_mate))
    keep_w = pltpu.make_async_copy(own_w, w_slot(t), local_sem.at[0])
    keep_c = pltpu.make_async_copy(c_ref, cg.at[l], local_sem.at[1])
    keep_w.start()
    keep_c.start()

    entries = cell_ref.shape[0]

    def fill(b, carry):
        r0 = pl.multiple_of(b * 16, 16)
        cell = cell_ref[pl.ds(r0, 16), :]
        at = lax.broadcasted_iota(jnp.int32, (16, cells), 1) - cell
        weights = weight_ref[pl.ds(r0, 16), :]
        total = jnp.zeros((16, cells), jnp.float32)
        for corner, offset in enumerate((0, 1, cols, cols + 1)):
            total = jnp.where(at == offset, weights[:, corner:corner + 1], total)
        spread_ref[pl.ds(r0, 16), :] = jnp.where(cell >= 0, total, 0.0).astype(jnp.bfloat16)
        return carry

    lax.fori_loop(0, entries // 16, fill, 0)
    keep_spread = pltpu.make_async_copy(spread_ref, spread_out, local_sem.at[2])
    keep_spread.start()
    col = lax.broadcasted_iota(jnp.int32, (cols, cols), 0)
    spot = lax.broadcasted_iota(jnp.int32, (cols, cols), 1)
    for r in range(rows_n):
        hit = ((col == 0) & (spot == r + 1)) | ((col == cols - 1) & (spot == cols // 2 + r + 1))
        sel_ref[r * cols:(r + 1) * cols, :] = jnp.where(hit, 1.0, 0.0).astype(jnp.bfloat16)

    def pass_w(k):
        index = t_of(t, -k)
        w_copy(0, k, index, own_w, t_of(t, k)).wait_recv()
        start(w_copy(1, k, index, w_slot(index), t_mate))

    def pass_c(ch):
        for k in range(1, half_l):
            index = l_of(l, -k)
            c_copy(0, k, ch, index, c_piece(c_ref, ch), l_of(l, k)).wait_recv()
            start(c_copy(1, k, ch, index, c_piece(cg.at[index], ch), l_mate))

    passed = 0
    for k in range(1, half_t):
        pass_w(k)
        while passed < chunks - 1 and passed * (half_t - 1) < k * (chunks - 1):
            pass_c(passed)
            passed += 1
    keep_w.wait()
    keep_c.wait()
    for k in range(half_t):
        w_copy(1, k, t_of(t_mate, -k), own_w, t_mate).wait_recv()

    rows = feat // 3
    span = width // cols
    kept = []

    def run_interior(ch):
        low = max(ch * span - 1, 0)
        high = rows_n if ch == chunks - 1 else (ch + 1) * span - 1

        def step(m, carry):
            part = pl.ds(pl.multiple_of(m * 128, 128), 128)
            interior(rows_n, cols, low, high, part, g_ref, k_ref, local_ref)
            return carry

        lax.fori_loop(0, feat // 128, step, 0)
        copy = pltpu.make_async_copy(
            local_ref.at[:, low * cols:high * cols], local_out.at[:, low * cols:high * cols],
            local_sem.at[3 + ch])
        copy.start()
        kept.append(copy)

    for ch in range(chunks):
        if ch >= passed:
            pass_c(ch)
        for k in range(half_l):
            c_copy(1, k, ch, l_of(l_mate, -k), c_piece(c_ref, ch), l_mate).wait_recv()

        def body(m, carry, ch=ch):
            r0 = pl.multiple_of(m * rows, rows)
            total = None
            if joined:
                for b in range(n_lev):
                    part = jnp.dot(wg[b, pl.ds(r0, rows), :], cg[b, :, ch * width:(ch + 1) * width],
                                   preferred_element_type=jnp.float32)
                    total = part if total is None else total + part
            else:
                for b in range(n_tile):
                    k0 = (b % per) * cb
                    part = jnp.dot(wg[b, pl.ds(r0, rows), :],
                                   cg[b // per, k0:k0 + cb, ch * width:(ch + 1) * width],
                                   preferred_element_type=jnp.float32)
                    total = part if total is None else total + part
            g_ref[pl.ds(r0, rows), ch * width:(ch + 1) * width] = total.astype(jnp.bfloat16)
            return carry

        lax.fori_loop(0, 3, body, 0)
        if ch < chunks - 1:
            run_interior(ch)

    strips = n_tile // 2
    q = lax.rem(t + strips // 2, n_tile)
    panel, place = q // strips, lax.rem(q, strips)
    keep_top = (place != 0).astype(jnp.float32)
    keep_bottom = (place != strips - 1).astype(jnp.float32)

    def shape(m, carry):
        edges(rows_n, cols, pl.ds(pl.multiple_of(m * 128, 128), 128), keep_top, keep_bottom,
              g_ref, k_ref, oh_ref, sel_ref, vals_ref, top_ref, bottom_ref)
        return carry

    lax.fori_loop(0, feat // 128, shape, 0)
    pad = entries // strips
    edge_copies = [
        pltpu.make_async_remote_copy(
            src_ref=top_ref, dst_ref=down_out, send_sem=es.at[0], recv_sem=er.at[0],
            device_id=(lax.rem(t + n_tile - 1, n_tile), l), device_id_type=MESH),
        pltpu.make_async_remote_copy(
            src_ref=bottom_ref, dst_ref=up_out, send_sem=es.at[1], recv_sem=er.at[1],
            device_id=(lax.rem(t + 1, n_tile), l), device_id_type=MESH),
    ]

    def vals_copy(j, slot):
        to = lax.rem((1 - panel) * strips + j - strips // 2 + n_tile, n_tile)
        return pltpu.make_async_remote_copy(
            src_ref=vals_ref.at[pl.ds(j * pad, pad)],
            dst_ref=vals_out.at[pl.ds(pl.multiple_of(slot * pad, 16), pad)],
            send_sem=es.at[2 + j], recv_sem=er.at[2 + slot], device_id=(to, l), device_id_type=MESH)

    for copy in edge_copies:
        start(copy)
    for j in range(strips):
        start(vals_copy(j, place))
    run_interior(chunks - 1)
    for copy in edge_copies:
        copy.wait_recv()
    for j in range(strips):
        vals_copy(j, j).wait_recv()
    keep_spread.wait()
    for copy in kept:
        copy.wait()
    for copy in sends:
        copy.wait_send()


def mix(c, w, kernel, picks, targets, weights, n_tile, n_lev, rows, cols):
    feat, cells = c.shape
    cb = w.shape[1]
    chunks = 4
    entries = picks.shape[0]
    strips = n_tile // 2
    w_shape = (n_lev, feat, feat) if cb % 128 == 0 else (n_tile, feat, cb)
    vmem = pl.BlockSpec(memory_space=pltpu.VMEM)
    anywhere = pl.BlockSpec(memory_space=pl.ANY)
    return pl.pallas_call(
        functools.partial(mix_kernel, n_tile, n_lev, chunks, rows, cols),
        out_shape=[
            jax.ShapeDtypeStruct((feat, cells), jnp.float32),
            jax.ShapeDtypeStruct((entries, feat), jnp.bfloat16),
            jax.ShapeDtypeStruct((feat, cols), jnp.bfloat16),
            jax.ShapeDtypeStruct((feat, cols), jnp.bfloat16),
            jax.ShapeDtypeStruct((entries, cells), jnp.bfloat16),
        ],
        in_specs=[anywhere] * 2 + [vmem] * 4,
        out_specs=[anywhere] * 5,
        scratch_shapes=[
            pltpu.VMEM((feat, cells), jnp.bfloat16),
            pltpu.VMEM((feat, cells), jnp.float32),
            pltpu.VMEM((entries, feat), jnp.bfloat16),
            pltpu.VMEM((feat, cols), jnp.bfloat16),
            pltpu.VMEM((feat, cols), jnp.bfloat16),
            pltpu.VMEM((entries, cells), jnp.bfloat16),
            pltpu.VMEM((cells, cols), jnp.bfloat16),
            pltpu.VMEM(w_shape, jnp.bfloat16),
            pltpu.VMEM((n_lev, feat, cells), jnp.bfloat16),
            pltpu.SemaphoreType.DMA((3 + chunks,)),
            pltpu.SemaphoreType.DMA((2, n_tile // 2)),
            pltpu.SemaphoreType.DMA((2, n_tile // 2)),
            pltpu.SemaphoreType.DMA((2, n_lev // 2, chunks)),
            pltpu.SemaphoreType.DMA((2, n_lev // 2, chunks)),
            pltpu.SemaphoreType.DMA((2 + strips,)),
            pltpu.SemaphoreType.DMA((2 + strips,)),
        ],
        compiler_params=pltpu.CompilerParams(
            collective_id=0, has_side_effects=True, vmem_limit_bytes=52 * 2**20),
        name="mix",
    )(c, w, kernel, picks, targets, weights)


def shifted(g_ref, part, r, cols):
    mid = g_ref[part, r * cols:(r + 1) * cols].astype(jnp.float32)
    lane = lax.broadcasted_iota(jnp.int32, mid.shape, 1)
    after = jnp.where(lane == cols - 1, 0.0, pltpu.roll(mid, cols - 1, 1))
    before = jnp.where(lane == 0, 0.0, pltpu.roll(mid, 1, 1))
    return after, mid, before


def taps_of(k_ref, part, cols):
    taps = k_ref[part, :]
    shape = (taps.shape[0], cols)
    return {(a, b): jnp.broadcast_to(taps[:, 3 * a + b + 4:3 * a + b + 5], shape)
            for a in (-1, 0, 1) for b in (-1, 0, 1)}


def row_part(weight, a, row):
    after, mid, before = row
    return weight[a, -1] * after + weight[a, 0] * mid + weight[a, 1] * before


def interior(rows, cols, low, high, part, g_ref, k_ref, local_ref):
    weight = taps_of(k_ref, part, cols)
    totals = {}
    for r in range(max(low - 1, 0), min(high + 1, rows)):
        row = shifted(g_ref, part, r, cols)
        for a in (-1, 0, 1):
            i = r + a
            if low <= i < high:
                value = row_part(weight, a, row)
                totals[i] = totals[i] + value if i in totals else value
        done = r - 1
        if done in totals:
            local_ref[part, done * cols:(done + 1) * cols] = totals.pop(done)
    for i, total in totals.items():
        local_ref[part, i * cols:(i + 1) * cols] = total


def edges(rows, cols, part, keep_top, keep_bottom,
          g_ref, k_ref, oh_ref, sel_ref, vals_ref, top_ref, bottom_ref):
    weight = taps_of(k_ref, part, cols)
    top = row_part(weight, -1, shifted(g_ref, part, 0, cols))
    bottom = row_part(weight, 1, shifted(g_ref, part, rows - 1, cols))
    top_ref[part, :] = (top * keep_top).astype(jnp.bfloat16)
    bottom_ref[part, :] = (bottom * keep_bottom).astype(jnp.bfloat16)
    edge = jnp.dot(g_ref[part, :], sel_ref[...], preferred_element_type=jnp.float32)
    near = lax.broadcasted_iota(jnp.int32, edge.shape, 1) < cols // 2
    sides = jnp.where(near, weight[0, -1], weight[0, 1]) * edge
    sides += jnp.where(near, weight[-1, -1], weight[-1, 1]) * pltpu.roll(edge, cols - 1, 1)
    sides += jnp.where(near, weight[1, -1], weight[1, 1]) * pltpu.roll(edge, 1, 1)
    cycle = jnp.concatenate([x.astype(jnp.bfloat16) for x in (top, bottom, sides)], axis=1)
    vals_ref[:, part] = lax.dot_general(
        oh_ref[...], cycle, (((1,), (1,)), ((), ())), preferred_element_type=jnp.float32
    ).astype(jnp.bfloat16)


def deposit_kernel(rows, cols, local_ref, vals_ref, spread_ref, up_ref, down_ref, out_ref):
    total = local_ref[...] + lax.dot_general(
        vals_ref[...], spread_ref[...], (((0,), (0,)), ((), ())), preferred_element_type=jnp.float32)
    first = total[:, :cols] + up_ref[...].astype(jnp.float32)
    last = total[:, -cols:] + down_ref[...].astype(jnp.float32)
    total = jnp.concatenate([first, total[:, cols:-cols], last], axis=1)
    out_ref[...] = total.reshape(total.shape[0], rows, cols).astype(jnp.bfloat16)


def slot_place(slot, rows, cols):
    side, far = 2 * cols, 2 * cols + cols // 2
    low = slot - (cols + 2)
    place = jnp.where(slot < cols + 2, slot - 1, cols + low - 1)
    place = jnp.where(slot == 0, side, place)
    place = jnp.where(slot == cols + 1, far, place)
    place = jnp.where(low == 0, side + rows + 1, place)
    place = jnp.where(low == cols + 1, far + rows + 1, place)
    left = slot - 2 * (cols + 2)
    place = jnp.where(left >= 0, side + 1 + left, place)
    place = jnp.where(left >= rows, far + 1 + left - rows, place)
    return jnp.where(slot < 0, -1, place)


def per_device(cotangent, mix_weight, kernel, send_rows, recv_cells, recv_weight, n_tile, n_lev):
    feat, rows, cols = cotangent.shape
    cells = rows * cols
    most = send_rows.shape[2]
    pad = -(-most // 16) * 16
    strips = n_tile // 2
    panel = (lax.axis_index("tile") + strips // 2) % n_tile // strips
    begin = ((1 - panel) * strips - strips // 2 + n_tile) % n_tile

    def of_partners(table, dim):
        table = lax.dynamic_slice_in_dim(jnp.concatenate([table, table], axis=dim), begin, strips, dim)
        width = [(0, 0)] * (table.ndim - 1) + [(0, pad - most)]
        return jnp.pad(table, width, constant_values=-1)

    places = slot_place(of_partners(send_rows[0], 0), rows, cols).reshape(-1, 1)
    picks = (places == jnp.arange(3 * cols, dtype=jnp.int32)[None, :]).astype(jnp.bfloat16)
    targets = of_partners(recv_cells[0], 0).reshape(-1, 1)
    weights = of_partners(recv_weight[0], 1).reshape(4, -1).T

    local, vals, up, down, spread = mix(
        cotangent.reshape(feat, cells), mix_weight, kernel, picks, targets, weights, n_tile, n_lev, rows, cols)

    fb = 128
    entries = picks.shape[0]
    grid = (feat // fb,)
    by_feat = lambda width: pl.BlockSpec((fb, width), lambda i: (i, 0))
    whole = lambda shape: pl.BlockSpec(shape, lambda i: (0, 0))
    by_column = pl.BlockSpec((entries, fb), lambda i: (0, i))
    params = pltpu.CompilerParams(vmem_limit_bytes=48 * 2**20)
    return pl.pallas_call(
        functools.partial(deposit_kernel, rows, cols),
        grid=grid,
        out_shape=jax.ShapeDtypeStruct((feat, rows, cols), jnp.bfloat16),
        in_specs=[by_feat(cells), by_column, whole((entries, cells)), by_feat(cols), by_feat(cols)],
        out_specs=pl.BlockSpec((fb, rows, cols), lambda i: (i, 0, 0)),
        compiler_params=params,
        name="deposit",
    )(local, vals, spread, up, down)


def solution(mesh):
    in_specs = (
        P("lev", "tile", None),
        P(None, "tile"),
        P("lev", None),
        P("tile", None, None),
        P("tile", None, None),
        P("tile", None, None, None),
    )
    return jax.shard_map(
        functools.partial(per_device, n_tile=mesh.shape["tile"], n_lev=mesh.shape["lev"]),
        mesh=mesh, in_specs=in_specs, out_specs=P("lev", "tile", None), check_vma=False)
```

```python
import functools

import jax
import jax.numpy as jnp
from jax import lax
from jax.experimental import pallas as pl
from jax.experimental.pallas import tpu as pltpu
from jax.sharding import PartitionSpec as P

MESH = pl.DeviceIdType.MESH


def mix_kernel(n_tile, n_lev, chunks, rows_n, cols, c_ref, w_ref, k_ref, oh_ref, cell_ref, weight_ref,
               local_out, vals_out, up_out, down_out, spread_out,
               g_ref, local_ref, vals_ref, top_ref, bottom_ref, spread_ref, sel_ref,
               wg, cg, local_sem, ws, wr, cs, cr, es, er):
    t = lax.axis_index("tile")
    l = lax.axis_index("lev")
    feat, cells = c_ref.shape
    cb = w_ref.shape[1]
    half_t, half_l = n_tile // 2, n_lev // 2
    width = cells // chunks
    per = feat // cb
    joined = len(wg.shape) == 3 and wg.shape[0] == n_lev and wg.shape[2] == feat
    t_mate = t + 1 - 2 * lax.rem(t, 2)
    l_mate = l + 1 - 2 * lax.rem(l, 2)

    def t_of(base, k):
        return lax.rem(base + 2 * k + 2 * n_tile, n_tile)

    def l_of(base, k):
        return lax.rem(base + 2 * k + 2 * n_lev, n_lev)

    barrier = pltpu.get_barrier_semaphore()
    peers = [(lax.rem(t + k, n_tile), l) for k in range(1, n_tile)] + [(t, l_mate)]
    peers += [(t, l_of(l, k)) for k in range(1, half_l)]
    for peer in peers:
        pl.semaphore_signal(barrier, inc=1, device_id=peer, device_id_type=MESH)
    pl.semaphore_wait(barrier, len(peers))

    def w_slot(index):
        if joined:
            return wg.at[index // per, :, pl.ds(pl.multiple_of(lax.rem(index, per) * cb, cb), cb)]
        return wg.at[index]

    own_w = w_ref.at[pl.ds(pl.multiple_of(l * feat, feat), feat)]

    def w_copy(lane, k, index, source, to):
        return pltpu.make_async_remote_copy(
            src_ref=source, dst_ref=w_slot(index), send_sem=ws.at[lane, k], recv_sem=wr.at[lane, k],
            device_id=(to, l), device_id_type=MESH)

    def c_piece(ref, ch):
        return ref.at[:, ch * width:(ch + 1) * width]

    def c_copy(lane, k, ch, index, source, to):
        return pltpu.make_async_remote_copy(
            src_ref=source, dst_ref=c_piece(cg.at[index], ch), send_sem=cs.at[lane, k, ch],
            recv_sem=cr.at[lane, k, ch], device_id=(t, to), device_id_type=MESH)

    sends = []

    def start(copy):
        copy.start()
        sends.append(copy)

    for k in range(1, half_t):
        start(w_copy(0, k, t, own_w, t_of(t, k)))
    start(w_copy(1, 0, t, own_w, t_mate))
    for ch in range(chunks):
        for k in range(1, half_l):
            start(c_copy(0, k, ch, l, c_piece(c_ref, ch), l_of(l, k)))
    for ch in range(chunks):
        start(c_copy(1, 0, ch, l, c_piece(c_ref, ch), l_mate))
    keep_w = pltpu.make_async_copy(own_w, w_slot(t), local_sem.at[0])
    keep_c = pltpu.make_async_copy(c_ref, cg.at[l], local_sem.at[1])
    keep_w.start()
    keep_c.start()

    entries = cell_ref.shape[0]

    def fill(b, carry):
        r0 = pl.multiple_of(b * 16, 16)
        cell = cell_ref[pl.ds(r0, 16), :]
        at = lax.broadcasted_iota(jnp.int32, (16, cells), 1) - cell
        weights = weight_ref[pl.ds(r0, 16), :]
        total = jnp.zeros((16, cells), jnp.float32)
        for corner, offset in enumerate((0, 1, cols, cols + 1)):
            total = jnp.where(at == offset, weights[:, corner:corner + 1], total)
        spread_ref[pl.ds(r0, 16), :] = jnp.where(cell >= 0, total, 0.0).astype(jnp.bfloat16)
        return carry

    lax.fori_loop(0, entries // 16, fill, 0)
    keep_spread = pltpu.make_async_copy(spread_ref, spread_out, local_sem.at[2])
    keep_spread.start()
    col = lax.broadcasted_iota(jnp.int32, (cols, cols), 0)
    spot = lax.broadcasted_iota(jnp.int32, (cols, cols), 1)
    for r in range(rows_n):
        hit = ((col == 0) & (spot == r + 1)) | ((col == cols - 1) & (spot == cols // 2 + r + 1))
        sel_ref[r * cols:(r + 1) * cols, :] = jnp.where(hit, 1.0, 0.0).astype(jnp.bfloat16)

    def pass_w(k):
        index = t_of(t, -k)
        w_copy(0, k, index, own_w, t_of(t, k)).wait_recv()
        start(w_copy(1, k, index, w_slot(index), t_mate))

    def pass_c(ch):
        for k in range(1, half_l):
            index = l_of(l, -k)
            c_copy(0, k, ch, index, c_piece(c_ref, ch), l_of(l, k)).wait_recv()
            start(c_copy(1, k, ch, index, c_piece(cg.at[index], ch), l_mate))

    for k in range(1, half_t):
        pass_w(k)
    keep_w.wait()
    keep_c.wait()
    for k in range(half_t):
        w_copy(1, k, t_of(t_mate, -k), own_w, t_mate).wait_recv()

    rows = feat // 3
    span = width // cols
    kept = []

    def run_interior(ch):
        low = max(ch * span - 1, 0)
        high = rows_n if ch == chunks - 1 else (ch + 1) * span - 1

        def step(m, carry):
            part = pl.ds(pl.multiple_of(m * 128, 128), 128)
            interior(rows_n, cols, low, high, part, g_ref, k_ref, local_ref)
            return carry

        lax.fori_loop(0, feat // 128, step, 0)
        copy = pltpu.make_async_copy(
            local_ref.at[:, low * cols:high * cols], local_out.at[:, low * cols:high * cols],
            local_sem.at[3 + ch])
        copy.start()
        kept.append(copy)

    for ch in range(chunks):
        pass_c(ch)
        for k in range(half_l):
            c_copy(1, k, ch, l_of(l_mate, -k), c_piece(c_ref, ch), l_mate).wait_recv()

        def body(m, carry, ch=ch):
            r0 = pl.multiple_of(m * rows, rows)
            total = None
            if joined:
                for b in range(n_lev):
                    part = jnp.dot(wg[b, pl.ds(r0, rows), :], cg[b, :, ch * width:(ch + 1) * width],
                                   preferred_element_type=jnp.float32)
                    total = part if total is None else total + part
            else:
                for b in range(n_tile):
                    k0 = (b % per) * cb
                    part = jnp.dot(wg[b, pl.ds(r0, rows), :],
                                   cg[b // per, k0:k0 + cb, ch * width:(ch + 1) * width],
                                   preferred_element_type=jnp.float32)
                    total = part if total is None else total + part
            g_ref[pl.ds(r0, rows), ch * width:(ch + 1) * width] = total.astype(jnp.bfloat16)
            return carry

        lax.fori_loop(0, 3, body, 0)
        if ch < chunks - 1:
            run_interior(ch)

    strips = n_tile // 2
    q = lax.rem(t + strips // 2, n_tile)
    panel, place = q // strips, lax.rem(q, strips)
    keep_top = (place != 0).astype(jnp.float32)
    keep_bottom = (place != strips - 1).astype(jnp.float32)

    def shape(m, carry):
        edges(rows_n, cols, pl.ds(pl.multiple_of(m * 128, 128), 128), keep_top, keep_bottom,
              g_ref, k_ref, oh_ref, sel_ref, vals_ref, top_ref, bottom_ref)
        return carry

    lax.fori_loop(0, feat // 128, shape, 0)
    pad = entries // strips
    edge_copies = [
        pltpu.make_async_remote_copy(
            src_ref=top_ref, dst_ref=down_out, send_sem=es.at[0], recv_sem=er.at[0],
            device_id=(lax.rem(t + n_tile - 1, n_tile), l), device_id_type=MESH),
        pltpu.make_async_remote_copy(
            src_ref=bottom_ref, dst_ref=up_out, send_sem=es.at[1], recv_sem=er.at[1],
            device_id=(lax.rem(t + 1, n_tile), l), device_id_type=MESH),
    ]

    def vals_copy(j, slot):
        to = lax.rem((1 - panel) * strips + j - strips // 2 + n_tile, n_tile)
        return pltpu.make_async_remote_copy(
            src_ref=vals_ref.at[pl.ds(j * pad, pad)],
            dst_ref=vals_out.at[pl.ds(pl.multiple_of(slot * pad, 16), pad)],
            send_sem=es.at[2 + j], recv_sem=er.at[2 + slot], device_id=(to, l), device_id_type=MESH)

    for copy in edge_copies:
        start(copy)
    for j in range(strips):
        start(vals_copy(j, place))
    run_interior(chunks - 1)
    for copy in edge_copies:
        copy.wait_recv()
    for j in range(strips):
        vals_copy(j, j).wait_recv()
    keep_spread.wait()
    for copy in kept:
        copy.wait()
    for copy in sends:
        copy.wait_send()


def mix(c, w, kernel, picks, targets, weights, n_tile, n_lev, rows, cols):
    feat, cells = c.shape
    cb = w.shape[1]
    chunks = 4
    entries = picks.shape[0]
    strips = n_tile // 2
    w_shape = (n_lev, feat, feat) if cb % 128 == 0 else (n_tile, feat, cb)
    vmem = pl.BlockSpec(memory_space=pltpu.VMEM)
    anywhere = pl.BlockSpec(memory_space=pl.ANY)
    return pl.pallas_call(
        functools.partial(mix_kernel, n_tile, n_lev, chunks, rows, cols),
        out_shape=[
            jax.ShapeDtypeStruct((feat, cells), jnp.float32),
            jax.ShapeDtypeStruct((entries, feat), jnp.bfloat16),
            jax.ShapeDtypeStruct((feat, cols), jnp.bfloat16),
            jax.ShapeDtypeStruct((feat, cols), jnp.bfloat16),
            jax.ShapeDtypeStruct((entries, cells), jnp.bfloat16),
        ],
        in_specs=[anywhere] * 2 + [vmem] * 4,
        out_specs=[anywhere] * 5,
        scratch_shapes=[
            pltpu.VMEM((feat, cells), jnp.bfloat16),
            pltpu.VMEM((feat, cells), jnp.float32),
            pltpu.VMEM((entries, feat), jnp.bfloat16),
            pltpu.VMEM((feat, cols), jnp.bfloat16),
            pltpu.VMEM((feat, cols), jnp.bfloat16),
            pltpu.VMEM((entries, cells), jnp.bfloat16),
            pltpu.VMEM((cells, cols), jnp.bfloat16),
            pltpu.VMEM(w_shape, jnp.bfloat16),
            pltpu.VMEM((n_lev, feat, cells), jnp.bfloat16),
            pltpu.SemaphoreType.DMA((3 + chunks,)),
            pltpu.SemaphoreType.DMA((2, n_tile // 2)),
            pltpu.SemaphoreType.DMA((2, n_tile // 2)),
            pltpu.SemaphoreType.DMA((2, n_lev // 2, chunks)),
            pltpu.SemaphoreType.DMA((2, n_lev // 2, chunks)),
            pltpu.SemaphoreType.DMA((2 + strips,)),
            pltpu.SemaphoreType.DMA((2 + strips,)),
        ],
        compiler_params=pltpu.CompilerParams(
            collective_id=0, has_side_effects=True, vmem_limit_bytes=52 * 2**20),
        name="mix",
    )(c, w, kernel, picks, targets, weights)


def shifted(g_ref, part, r, cols):
    mid = g_ref[part, r * cols:(r + 1) * cols].astype(jnp.float32)
    lane = lax.broadcasted_iota(jnp.int32, mid.shape, 1)
    after = jnp.where(lane == cols - 1, 0.0, pltpu.roll(mid, cols - 1, 1))
    before = jnp.where(lane == 0, 0.0, pltpu.roll(mid, 1, 1))
    return after, mid, before


def taps_of(k_ref, part, cols):
    taps = k_ref[part, :]
    shape = (taps.shape[0], cols)
    return {(a, b): jnp.broadcast_to(taps[:, 3 * a + b + 4:3 * a + b + 5], shape)
            for a in (-1, 0, 1) for b in (-1, 0, 1)}


def row_part(weight, a, row):
    after, mid, before = row
    return weight[a, -1] * after + weight[a, 0] * mid + weight[a, 1] * before


def interior(rows, cols, low, high, part, g_ref, k_ref, local_ref):
    weight = taps_of(k_ref, part, cols)
    totals = {}
    for r in range(max(low - 1, 0), min(high + 1, rows)):
        row = shifted(g_ref, part, r, cols)
        for a in (-1, 0, 1):
            i = r + a
            if low <= i < high:
                value = row_part(weight, a, row)
                totals[i] = totals[i] + value if i in totals else value
        done = r - 1
        if done in totals:
            local_ref[part, done * cols:(done + 1) * cols] = totals.pop(done)
    for i, total in totals.items():
        local_ref[part, i * cols:(i + 1) * cols] = total


def edges(rows, cols, part, keep_top, keep_bottom,
          g_ref, k_ref, oh_ref, sel_ref, vals_ref, top_ref, bottom_ref):
    weight = taps_of(k_ref, part, cols)
    top = row_part(weight, -1, shifted(g_ref, part, 0, cols))
    bottom = row_part(weight, 1, shifted(g_ref, part, rows - 1, cols))
    top_ref[part, :] = (top * keep_top).astype(jnp.bfloat16)
    bottom_ref[part, :] = (bottom * keep_bottom).astype(jnp.bfloat16)
    edge = jnp.dot(g_ref[part, :], sel_ref[...], preferred_element_type=jnp.float32)
    near = lax.broadcasted_iota(jnp.int32, edge.shape, 1) < cols // 2
    sides = jnp.where(near, weight[0, -1], weight[0, 1]) * edge
    sides += jnp.where(near, weight[-1, -1], weight[-1, 1]) * pltpu.roll(edge, cols - 1, 1)
    sides += jnp.where(near, weight[1, -1], weight[1, 1]) * pltpu.roll(edge, 1, 1)
    cycle = jnp.concatenate([x.astype(jnp.bfloat16) for x in (top, bottom, sides)], axis=1)
    vals_ref[:, part] = lax.dot_general(
        oh_ref[...], cycle, (((1,), (1,)), ((), ())), preferred_element_type=jnp.float32
    ).astype(jnp.bfloat16)


def deposit_kernel(rows, cols, local_ref, vals_ref, spread_ref, up_ref, down_ref, out_ref):
    total = local_ref[...] + lax.dot_general(
        vals_ref[...], spread_ref[...], (((0,), (0,)), ((), ())), preferred_element_type=jnp.float32)
    first = total[:, :cols] + up_ref[...].astype(jnp.float32)
    last = total[:, -cols:] + down_ref[...].astype(jnp.float32)
    total = jnp.concatenate([first, total[:, cols:-cols], last], axis=1)
    out_ref[...] = total.reshape(total.shape[0], rows, cols).astype(jnp.bfloat16)


def slot_place(slot, rows, cols):
    side, far = 2 * cols, 2 * cols + cols // 2
    low = slot - (cols + 2)
    place = jnp.where(slot < cols + 2, slot - 1, cols + low - 1)
    place = jnp.where(slot == 0, side, place)
    place = jnp.where(slot == cols + 1, far, place)
    place = jnp.where(low == 0, side + rows + 1, place)
    place = jnp.where(low == cols + 1, far + rows + 1, place)
    left = slot - 2 * (cols + 2)
    place = jnp.where(left >= 0, side + 1 + left, place)
    place = jnp.where(left >= rows, far + 1 + left - rows, place)
    return jnp.where(slot < 0, -1, place)


def per_device(cotangent, mix_weight, kernel, send_rows, recv_cells, recv_weight, n_tile, n_lev):
    feat, rows, cols = cotangent.shape
    cells = rows * cols
    most = send_rows.shape[2]
    pad = -(-most // 16) * 16
    strips = n_tile // 2
    panel = (lax.axis_index("tile") + strips // 2) % n_tile // strips
    begin = ((1 - panel) * strips - strips // 2 + n_tile) % n_tile

    def of_partners(table, dim):
        table = lax.dynamic_slice_in_dim(jnp.concatenate([table, table], axis=dim), begin, strips, dim)
        width = [(0, 0)] * (table.ndim - 1) + [(0, pad - most)]
        return jnp.pad(table, width, constant_values=-1)

    places = slot_place(of_partners(send_rows[0], 0), rows, cols).reshape(-1, 1)
    picks = (places == jnp.arange(3 * cols, dtype=jnp.int32)[None, :]).astype(jnp.bfloat16)
    targets = of_partners(recv_cells[0], 0).reshape(-1, 1)
    weights = of_partners(recv_weight[0], 1).reshape(4, -1).T

    local, vals, up, down, spread = mix(
        cotangent.reshape(feat, cells), mix_weight, kernel, picks, targets, weights, n_tile, n_lev, rows, cols)

    fb = 128
    entries = picks.shape[0]
    grid = (feat // fb,)
    by_feat = lambda width: pl.BlockSpec((fb, width), lambda i: (i, 0))
    whole = lambda shape: pl.BlockSpec(shape, lambda i: (0, 0))
    by_column = pl.BlockSpec((entries, fb), lambda i: (0, i))
    params = pltpu.CompilerParams(vmem_limit_bytes=48 * 2**20)
    return pl.pallas_call(
        functools.partial(deposit_kernel, rows, cols),
        grid=grid,
        out_shape=jax.ShapeDtypeStruct((feat, rows, cols), jnp.bfloat16),
        in_specs=[by_feat(cells), by_column, whole((entries, cells)), by_feat(cols), by_feat(cols)],
        out_specs=pl.BlockSpec((fb, rows, cols), lambda i: (i, 0, 0)),
        compiler_params=params,
        name="deposit",
    )(local, vals, spread, up, down)


def solution(mesh):
    in_specs = (
        P("lev", "tile", None),
        P(None, "tile"),
        P("lev", None),
        P("tile", None, None),
        P("tile", None, None),
        P("tile", None, None, None),
    )
    return jax.shard_map(
        functools.partial(per_device, n_tile=mesh.shape["tile"], n_lev=mesh.shape["lev"]),
        mesh=mesh, in_specs=in_specs, out_specs=P("lev", "tile", None), check_vma=False)
```

```python
import functools

import jax
import jax.numpy as jnp
from jax import lax
from jax.experimental import pallas as pl
from jax.experimental.pallas import tpu as pltpu
from jax.sharding import PartitionSpec as P

MESH = pl.DeviceIdType.MESH


def mix_kernel(n_tile, n_lev, chunks, rows_n, cols, c_ref, w_ref, k_ref, oh_ref, cell_ref, weight_ref,
               local_out, vals_out, up_out, down_out, spread_out,
               g_ref, local_ref, vals_ref, top_ref, bottom_ref, spread_ref, sel_ref,
               wg, cg, local_sem, ws, wr, cs, cr, es, er):
    t = lax.axis_index("tile")
    l = lax.axis_index("lev")
    feat, cells = c_ref.shape
    cb = w_ref.shape[1]
    half_t, half_l = n_tile // 2, n_lev // 2
    width = cells // chunks
    per = feat // cb
    joined = len(wg.shape) == 3 and wg.shape[0] == n_lev and wg.shape[2] == feat
    t_mate = t + 1 - 2 * lax.rem(t, 2)
    l_mate = l + 1 - 2 * lax.rem(l, 2)

    def t_of(base, k):
        return lax.rem(base + 2 * k + 2 * n_tile, n_tile)

    def l_of(base, k):
        return lax.rem(base + 2 * k + 2 * n_lev, n_lev)

    barrier = pltpu.get_barrier_semaphore()
    peers = [(lax.rem(t + k, n_tile), l) for k in range(1, n_tile)] + [(t, l_mate)]
    peers += [(t, l_of(l, k)) for k in range(1, half_l)]
    for peer in peers:
        pl.semaphore_signal(barrier, inc=1, device_id=peer, device_id_type=MESH)
    pl.semaphore_wait(barrier, len(peers))

    def w_slot(index):
        if joined:
            return wg.at[index // per, :, pl.ds(pl.multiple_of(lax.rem(index, per) * cb, cb), cb)]
        return wg.at[index]

    own_w = w_ref.at[pl.ds(pl.multiple_of(l * feat, feat), feat)]

    def w_copy(lane, k, index, source, to):
        return pltpu.make_async_remote_copy(
            src_ref=source, dst_ref=w_slot(index), send_sem=ws.at[lane, k], recv_sem=wr.at[lane, k],
            device_id=(to, l), device_id_type=MESH)

    def c_piece(ref, ch):
        return ref.at[:, ch * width:(ch + 1) * width]

    def c_copy(lane, k, ch, index, source, to):
        return pltpu.make_async_remote_copy(
            src_ref=source, dst_ref=c_piece(cg.at[index], ch), send_sem=cs.at[lane, k, ch],
            recv_sem=cr.at[lane, k, ch], device_id=(t, to), device_id_type=MESH)

    sends = []

    def start(copy):
        copy.start()
        sends.append(copy)

    for ch in range(chunks):
        for k in range(1, half_l):
            start(c_copy(0, k, ch, l, c_piece(c_ref, ch), l_of(l, k)))
    for k in range(1, half_t):
        start(w_copy(0, k, t, own_w, t_of(t, k)))
    start(w_copy(1, 0, t, own_w, t_mate))
    for ch in range(chunks):
        start(c_copy(1, 0, ch, l, c_piece(c_ref, ch), l_mate))
    keep_w = pltpu.make_async_copy(own_w, w_slot(t), local_sem.at[0])
    keep_c = pltpu.make_async_copy(c_ref, cg.at[l], local_sem.at[1])
    keep_w.start()
    keep_c.start()

    entries = cell_ref.shape[0]

    def fill(b, carry):
        r0 = pl.multiple_of(b * 16, 16)
        cell = cell_ref[pl.ds(r0, 16), :]
        at = lax.broadcasted_iota(jnp.int32, (16, cells), 1) - cell
        weights = weight_ref[pl.ds(r0, 16), :]
        total = jnp.zeros((16, cells), jnp.float32)
        for corner, offset in enumerate((0, 1, cols, cols + 1)):
            total = jnp.where(at == offset, weights[:, corner:corner + 1], total)
        spread_ref[pl.ds(r0, 16), :] = jnp.where(cell >= 0, total, 0.0).astype(jnp.bfloat16)
        return carry

    lax.fori_loop(0, entries // 16, fill, 0)
    keep_spread = pltpu.make_async_copy(spread_ref, spread_out, local_sem.at[2])
    keep_spread.start()
    col = lax.broadcasted_iota(jnp.int32, (cols, cols), 0)
    spot = lax.broadcasted_iota(jnp.int32, (cols, cols), 1)
    for r in range(rows_n):
        hit = ((col == 0) & (spot == r + 1)) | ((col == cols - 1) & (spot == cols // 2 + r + 1))
        sel_ref[r * cols:(r + 1) * cols, :] = jnp.where(hit, 1.0, 0.0).astype(jnp.bfloat16)

    def pass_w(k):
        index = t_of(t, -k)
        w_copy(0, k, index, own_w, t_of(t, k)).wait_recv()
        start(w_copy(1, k, index, w_slot(index), t_mate))

    def pass_c(ch):
        for k in range(1, half_l):
            index = l_of(l, -k)
            c_copy(0, k, ch, index, c_piece(c_ref, ch), l_of(l, k)).wait_recv()
            start(c_copy(1, k, ch, index, c_piece(cg.at[index], ch), l_mate))

    passed = 0
    for k in range(1, half_t):
        pass_w(k)
        while passed < chunks - 1 and passed * (half_t - 1) < k * (chunks - 1):
            pass_c(passed)
            passed += 1
    keep_w.wait()
    keep_c.wait()
    for k in range(half_t):
        w_copy(1, k, t_of(t_mate, -k), own_w, t_mate).wait_recv()

    rows = feat // 3
    kept = []

    def run_interior(ch):
        low, high = 0, rows_n

        def step(m, carry):
            part = pl.ds(pl.multiple_of(m * 128, 128), 128)
            interior(rows_n, cols, low, high, part, g_ref, k_ref, local_ref)
            return carry

        lax.fori_loop(0, feat // 128, step, 0)
        copy = pltpu.make_async_copy(
            local_ref.at[:, low * cols:high * cols], local_out.at[:, low * cols:high * cols],
            local_sem.at[3 + ch])
        copy.start()
        kept.append(copy)

    for ch in range(chunks):
        if ch >= passed:
            pass_c(ch)
        for k in range(half_l):
            c_copy(1, k, ch, l_of(l_mate, -k), c_piece(c_ref, ch), l_mate).wait_recv()

        def body(m, carry, ch=ch):
            r0 = pl.multiple_of(m * rows, rows)
            total = None
            if joined:
                for b in range(n_lev):
                    part = jnp.dot(wg[b, pl.ds(r0, rows), :], cg[b, :, ch * width:(ch + 1) * width],
                                   preferred_element_type=jnp.float32)
                    total = part if total is None else total + part
            else:
                for b in range(n_tile):
                    k0 = (b % per) * cb
                    part = jnp.dot(wg[b, pl.ds(r0, rows), :],
                                   cg[b // per, k0:k0 + cb, ch * width:(ch + 1) * width],
                                   preferred_element_type=jnp.float32)
                    total = part if total is None else total + part
            g_ref[pl.ds(r0, rows), ch * width:(ch + 1) * width] = total.astype(jnp.bfloat16)
            return carry

        lax.fori_loop(0, 3, body, 0)

    strips = n_tile // 2
    q = lax.rem(t + strips // 2, n_tile)
    panel, place = q // strips, lax.rem(q, strips)
    keep_top = (place != 0).astype(jnp.float32)
    keep_bottom = (place != strips - 1).astype(jnp.float32)

    def shape(m, carry):
        edges(rows_n, cols, pl.ds(pl.multiple_of(m * 128, 128), 128), keep_top, keep_bottom,
              g_ref, k_ref, oh_ref, sel_ref, vals_ref, top_ref, bottom_ref)
        return carry

    lax.fori_loop(0, feat // 128, shape, 0)
    pad = entries // strips
    edge_copies = [
        pltpu.make_async_remote_copy(
            src_ref=top_ref, dst_ref=down_out, send_sem=es.at[0], recv_sem=er.at[0],
            device_id=(lax.rem(t + n_tile - 1, n_tile), l), device_id_type=MESH),
        pltpu.make_async_remote_copy(
            src_ref=bottom_ref, dst_ref=up_out, send_sem=es.at[1], recv_sem=er.at[1],
            device_id=(lax.rem(t + 1, n_tile), l), device_id_type=MESH),
    ]

    def vals_copy(j, slot):
        to = lax.rem((1 - panel) * strips + j - strips // 2 + n_tile, n_tile)
        return pltpu.make_async_remote_copy(
            src_ref=vals_ref.at[pl.ds(j * pad, pad)],
            dst_ref=vals_out.at[pl.ds(pl.multiple_of(slot * pad, 16), pad)],
            send_sem=es.at[2 + j], recv_sem=er.at[2 + slot], device_id=(to, l), device_id_type=MESH)

    for copy in edge_copies:
        start(copy)
    for j in range(strips):
        start(vals_copy(j, place))
    run_interior(chunks - 1)
    for copy in edge_copies:
        copy.wait_recv()
    for j in range(strips):
        vals_copy(j, j).wait_recv()
    keep_spread.wait()
    for copy in kept:
        copy.wait()
    for copy in sends:
        copy.wait_send()


def mix(c, w, kernel, picks, targets, weights, n_tile, n_lev, rows, cols):
    feat, cells = c.shape
    cb = w.shape[1]
    chunks = 4
    entries = picks.shape[0]
    strips = n_tile // 2
    w_shape = (n_lev, feat, feat) if cb % 128 == 0 else (n_tile, feat, cb)
    vmem = pl.BlockSpec(memory_space=pltpu.VMEM)
    anywhere = pl.BlockSpec(memory_space=pl.ANY)
    return pl.pallas_call(
        functools.partial(mix_kernel, n_tile, n_lev, chunks, rows, cols),
        out_shape=[
            jax.ShapeDtypeStruct((feat, cells), jnp.float32),
            jax.ShapeDtypeStruct((entries, feat), jnp.bfloat16),
            jax.ShapeDtypeStruct((feat, cols), jnp.bfloat16),
            jax.ShapeDtypeStruct((feat, cols), jnp.bfloat16),
            jax.ShapeDtypeStruct((entries, cells), jnp.bfloat16),
        ],
        in_specs=[anywhere] * 2 + [vmem] * 4,
        out_specs=[anywhere] * 5,
        scratch_shapes=[
            pltpu.VMEM((feat, cells), jnp.bfloat16),
            pltpu.VMEM((feat, cells), jnp.float32),
            pltpu.VMEM((entries, feat), jnp.bfloat16),
            pltpu.VMEM((feat, cols), jnp.bfloat16),
            pltpu.VMEM((feat, cols), jnp.bfloat16),
            pltpu.VMEM((entries, cells), jnp.bfloat16),
            pltpu.VMEM((cells, cols), jnp.bfloat16),
            pltpu.VMEM(w_shape, jnp.bfloat16),
            pltpu.VMEM((n_lev, feat, cells), jnp.bfloat16),
            pltpu.SemaphoreType.DMA((3 + chunks,)),
            pltpu.SemaphoreType.DMA((2, n_tile // 2)),
            pltpu.SemaphoreType.DMA((2, n_tile // 2)),
            pltpu.SemaphoreType.DMA((2, n_lev // 2, chunks)),
            pltpu.SemaphoreType.DMA((2, n_lev // 2, chunks)),
            pltpu.SemaphoreType.DMA((2 + strips,)),
            pltpu.SemaphoreType.DMA((2 + strips,)),
        ],
        compiler_params=pltpu.CompilerParams(
            collective_id=0, has_side_effects=True, vmem_limit_bytes=52 * 2**20),
        name="mix",
    )(c, w, kernel, picks, targets, weights)


def shifted(g_ref, part, r, cols):
    mid = g_ref[part, r * cols:(r + 1) * cols].astype(jnp.float32)
    lane = lax.broadcasted_iota(jnp.int32, mid.shape, 1)
    after = jnp.where(lane == cols - 1, 0.0, pltpu.roll(mid, cols - 1, 1))
    before = jnp.where(lane == 0, 0.0, pltpu.roll(mid, 1, 1))
    return after, mid, before


def taps_of(k_ref, part, cols):
    taps = k_ref[part, :]
    shape = (taps.shape[0], cols)
    return {(a, b): jnp.broadcast_to(taps[:, 3 * a + b + 4:3 * a + b + 5], shape)
            for a in (-1, 0, 1) for b in (-1, 0, 1)}


def row_part(weight, a, row):
    after, mid, before = row
    return weight[a, -1] * after + weight[a, 0] * mid + weight[a, 1] * before


def interior(rows, cols, low, high, part, g_ref, k_ref, local_ref):
    weight = taps_of(k_ref, part, cols)
    totals = {}
    for r in range(max(low - 1, 0), min(high + 1, rows)):
        row = shifted(g_ref, part, r, cols)
        for a in (-1, 0, 1):
            i = r + a
            if low <= i < high:
                value = row_part(weight, a, row)
                totals[i] = totals[i] + value if i in totals else value
        done = r - 1
        if done in totals:
            local_ref[part, done * cols:(done + 1) * cols] = totals.pop(done)
    for i, total in totals.items():
        local_ref[part, i * cols:(i + 1) * cols] = total


def edges(rows, cols, part, keep_top, keep_bottom,
          g_ref, k_ref, oh_ref, sel_ref, vals_ref, top_ref, bottom_ref):
    weight = taps_of(k_ref, part, cols)
    top = row_part(weight, -1, shifted(g_ref, part, 0, cols))
    bottom = row_part(weight, 1, shifted(g_ref, part, rows - 1, cols))
    top_ref[part, :] = (top * keep_top).astype(jnp.bfloat16)
    bottom_ref[part, :] = (bottom * keep_bottom).astype(jnp.bfloat16)
    edge = jnp.dot(g_ref[part, :], sel_ref[...], preferred_element_type=jnp.float32)
    near = lax.broadcasted_iota(jnp.int32, edge.shape, 1) < cols // 2
    sides = jnp.where(near, weight[0, -1], weight[0, 1]) * edge
    sides += jnp.where(near, weight[-1, -1], weight[-1, 1]) * pltpu.roll(edge, cols - 1, 1)
    sides += jnp.where(near, weight[1, -1], weight[1, 1]) * pltpu.roll(edge, 1, 1)
    cycle = jnp.concatenate([x.astype(jnp.bfloat16) for x in (top, bottom, sides)], axis=1)
    vals_ref[:, part] = lax.dot_general(
        oh_ref[...], cycle, (((1,), (1,)), ((), ())), preferred_element_type=jnp.float32
    ).astype(jnp.bfloat16)


def deposit_kernel(rows, cols, local_ref, vals_ref, spread_ref, up_ref, down_ref, out_ref):
    total = local_ref[...] + lax.dot_general(
        vals_ref[...], spread_ref[...], (((0,), (0,)), ((), ())), preferred_element_type=jnp.float32)
    first = total[:, :cols] + up_ref[...].astype(jnp.float32)
    last = total[:, -cols:] + down_ref[...].astype(jnp.float32)
    total = jnp.concatenate([first, total[:, cols:-cols], last], axis=1)
    out_ref[...] = total.reshape(total.shape[0], rows, cols).astype(jnp.bfloat16)


def slot_place(slot, rows, cols):
    side, far = 2 * cols, 2 * cols + cols // 2
    low = slot - (cols + 2)
    place = jnp.where(slot < cols + 2, slot - 1, cols + low - 1)
    place = jnp.where(slot == 0, side, place)
    place = jnp.where(slot == cols + 1, far, place)
    place = jnp.where(low == 0, side + rows + 1, place)
    place = jnp.where(low == cols + 1, far + rows + 1, place)
    left = slot - 2 * (cols + 2)
    place = jnp.where(left >= 0, side + 1 + left, place)
    place = jnp.where(left >= rows, far + 1 + left - rows, place)
    return jnp.where(slot < 0, -1, place)


def per_device(cotangent, mix_weight, kernel, send_rows, recv_cells, recv_weight, n_tile, n_lev):
    feat, rows, cols = cotangent.shape
    cells = rows * cols
    most = send_rows.shape[2]
    pad = -(-most // 16) * 16
    strips = n_tile // 2
    panel = (lax.axis_index("tile") + strips // 2) % n_tile // strips
    begin = ((1 - panel) * strips - strips // 2 + n_tile) % n_tile

    def of_partners(table, dim):
        table = lax.dynamic_slice_in_dim(jnp.concatenate([table, table], axis=dim), begin, strips, dim)
        width = [(0, 0)] * (table.ndim - 1) + [(0, pad - most)]
        return jnp.pad(table, width, constant_values=-1)

    places = slot_place(of_partners(send_rows[0], 0), rows, cols).reshape(-1, 1)
    picks = (places == jnp.arange(3 * cols, dtype=jnp.int32)[None, :]).astype(jnp.bfloat16)
    targets = of_partners(recv_cells[0], 0).reshape(-1, 1)
    weights = of_partners(recv_weight[0], 1).reshape(4, -1).T

    local, vals, up, down, spread = mix(
        cotangent.reshape(feat, cells), mix_weight, kernel, picks, targets, weights, n_tile, n_lev, rows, cols)

    fb = 128
    entries = picks.shape[0]
    grid = (feat // fb,)
    by_feat = lambda width: pl.BlockSpec((fb, width), lambda i: (i, 0))
    whole = lambda shape: pl.BlockSpec(shape, lambda i: (0, 0))
    by_column = pl.BlockSpec((entries, fb), lambda i: (0, i))
    params = pltpu.CompilerParams(vmem_limit_bytes=48 * 2**20)
    return pl.pallas_call(
        functools.partial(deposit_kernel, rows, cols),
        grid=grid,
        out_shape=jax.ShapeDtypeStruct((feat, rows, cols), jnp.bfloat16),
        in_specs=[by_feat(cells), by_column, whole((entries, cells)), by_feat(cols), by_feat(cols)],
        out_specs=pl.BlockSpec((fb, rows, cols), lambda i: (i, 0, 0)),
        compiler_params=params,
        name="deposit",
    )(local, vals, spread, up, down)


def solution(mesh):
    in_specs = (
        P("lev", "tile", None),
        P(None, "tile"),
        P("lev", None),
        P("tile", None, None),
        P("tile", None, None),
        P("tile", None, None, None),
    )
    return jax.shard_map(
        functools.partial(per_device, n_tile=mesh.shape["tile"], n_lev=mesh.shape["lev"]),
        mesh=mesh, in_specs=in_specs, out_specs=P("lev", "tile", None), check_vma=False)
```
